32 devices in a mesh: rep: 4 (over y, x), shard: 8 (over z, core).
Axes of the slice: x: 2, y: 2, z: 4, core: 2. Of those that a mesh axis runs over, the one named last changes fastest.
Arguments:
- local_dense: float32 [4, 1024, 1024], P('rep', 'shard'), may hold values from -6 to 6
- anchor_dense: float32 [1024, 1024], P('shard'), may hold values from -6 to 6
- momentum_dense: float32 [1024, 1024], P('shard'), may hold values from -6 to 6
- local_emb: float32 [4, 8192, 2048], P('rep', 'shard'), may hold values from -24 to 24
- anchor_emb: float32 [8192, 2048], P('shard'), may hold values from -24 to 24
- momentum_emb: float32 [8192, 2048], P('shard'), may hold values from -6 to 6
- proj_basis: float32 [2048, 64], P('shard'), may hold values from -6 to 6
Outputs:
- new_dense_anchor: float32 [1024, 1024], P('shard')
- new_dense_momentum: float32 [1024, 1024], P('shard')
- dense_weights: bfloat16 [1024, 1024], replicated
- new_emb_anchor: float32 [8192, 2048], P('shard')
- new_emb_momentum: float32 [8192, 2048], P('shard')
The draws below stay inside these ranges and needn't reach their ends.
All inputs are finite; a program needn't handle non-finite values.
Results may differ from the reference program's by a relative error of at most 0.0004.
Values may be sent and summed in bfloat16 or wider, within the bound.
A program may use at most 128 MiB of HBM per device.

```python
import math
import jax
import jax.numpy as jnp
from jax import lax

D = 2048
DIN = 1024
DOUT = 1024
VOCAB = 8192
RANK = 64
REPS = 4


def row_gains(key):
    positions = jnp.arange(VOCAB, dtype=jnp.float32)
    rising = 0.3 * 3.0 ** (positions / max(VOCAB - 1, 1))
    spread = math.log(3.3)
    rough_part = jnp.exp(jax.random.uniform(jax.random.fold_in(key, 11), (VOCAB,), jnp.float32, 0.0, spread))
    return rising * rough_part


def noise_block(noise_key, shape):
    return jnp.clip(jax.random.normal(noise_key, shape, jnp.float32), -5.0, 5.0)


def draw_local_emb(key, part):
    gain_rows = row_gains(key)
    values = noise_block(jax.random.fold_in(key, 23), (REPS, VOCAB, D))
    return values * gain_rows[None, :, None]


def draw_anchor_emb(key, part):
    gain_rows = row_gains(key)
    values = noise_block(jax.random.fold_in(key, 29), (VOCAB, D))
    return values * gain_rows[:, None]


def block_scale(key, extent, shards, low, high):
    def one(axis_at, shards_of):
        draws = jax.random.uniform(jax.random.fold_in(jax.random.fold_in(key, 6), axis_at), (shards_of,), jnp.float32, low / len(shards), high / len(shards))
        return jnp.repeat(jnp.exp(draws), extent[axis_at] // shards_of).reshape((-1,) + (1,) * (len(extent) - axis_at - 1))

    level = one(*shards[0])
    for cut in shards[1:]:
        level = level * one(*cut)
    return level


def centred(key, shape, deviation, limit, shards=(), held_as=jnp.bfloat16):
    array = jax.random.normal(key, shape, jnp.float32) * deviation
    if len(shards) > 0:
        array = block_scale(key, shape, shards, -0.22, 0.18) * array
    return jnp.clip(array, min=-limit, max=limit).astype(held_as)


def setup_inputs(seed: int = 0) -> dict:
    keys = jax.random.split(jax.random.key(seed), 8)
    return {
        "local_dense": centred(keys[0], (REPS, DIN, DOUT), 1.0, 6.0, ((0, 4), (1, 8)), jnp.float32),
        "anchor_dense": centred(keys[1], (DIN, DOUT), 1.0, 6.0, ((0, 8),), jnp.float32),
        "momentum_dense": centred(keys[2], (DIN, DOUT), 0.5, 6.0, ((0, 8),), jnp.float32),
        "local_emb": draw_local_emb(jax.random.fold_in(keys[7], 71), 0),
        "anchor_emb": draw_anchor_emb(jax.random.fold_in(keys[7], 71), 0),
        "momentum_emb": centred(keys[5], (VOCAB, D), 0.5, 6.0, ((0, 8),), jnp.float32),
        "proj_basis": centred(keys[6], (D, RANK), 1.0, 6.0, ((0, 8),), jnp.float32),
    }


outer_rate = 0.7
momentum_rate = 0.9
highest = lax.Precision.HIGHEST

def reference(local_dense, anchor_dense, momentum_dense, local_emb, anchor_emb, momentum_emb, proj_basis):
    dense_grad = jnp.sum(anchor_dense[None] - local_dense, axis=0) / REPS
    dense_mom = momentum_rate * momentum_dense + dense_grad
    dense_new = anchor_dense - outer_rate * (dense_grad + momentum_rate * dense_mom)
    dense_weights = dense_new.astype(jnp.bfloat16)
    factor = jnp.zeros((VOCAB, RANK), jnp.float32)
    for replica in range(REPS):
        emb_diff = anchor_emb - local_emb[replica]
        factor = factor + jnp.dot(emb_diff.astype(jnp.float32), proj_basis.astype(jnp.float32), precision=highest, preferred_element_type=jnp.float32)
    gram_matrix = lax.dot_general(factor.astype(jnp.float32), factor.astype(jnp.float32), (((0,), (0,)), ((), ())), precision=highest, preferred_element_type=jnp.float32)
    chol_lower = jnp.linalg.cholesky(gram_matrix)
    ortho_rows = jax.scipy.linalg.solve_triangular(chol_lower, factor.T, lower=True).T
    coefficients = jnp.zeros((D, RANK), jnp.float32)
    for replica in range(REPS):
        emb_diff = anchor_emb - local_emb[replica]
        coefficients = coefficients + lax.dot_general(emb_diff.astype(jnp.float32), ortho_rows.astype(jnp.float32), (((0,), (0,)), ((), ())), precision=highest, preferred_element_type=jnp.float32)
    emb_grad = lax.dot_general(ortho_rows.astype(jnp.float32), coefficients.astype(jnp.float32), (((1,), (1,)), ((), ())), precision=highest, preferred_element_type=jnp.float32) / REPS
    emb_mom = momentum_rate * momentum_emb + emb_grad
    emb_new = anchor_emb - outer_rate * (emb_grad + momentum_rate * emb_mom)
    return (dense_new, dense_mom, dense_weights, emb_new, emb_mom)
```

```python
import functools

import jax
import jax.numpy as jnp
from jax import lax
from jax.experimental import pallas as pl
from jax.experimental.pallas import tpu as pltpu
from jax.sharding import PartitionSpec as P

outer_rate = 0.7
momentum_rate = 0.9
highest = lax.Precision.HIGHEST
f32 = jnp.float32
bf16 = jnp.bfloat16
MESH = pl.DeviceIdType.MESH


def nesterov(grad, anchor, momentum):
    mom = momentum_rate * momentum + grad
    return anchor - outer_rate * (grad + momentum_rate * mom), mom


def plain(local_dense, anchor_dense, momentum_dense, local_emb, anchor_emb, momentum_emb, proj_basis):
    groups = lax.axis_size("rep")
    basis = lax.all_gather(proj_basis, "shard", axis=0, tiled=True)
    diff = anchor_emb - local_emb[0]
    part = jnp.dot(diff, basis, precision=highest, preferred_element_type=f32)
    dense_sum, factor = lax.psum((anchor_dense - local_dense[0], part), "rep")
    dense_new, dense_mom = nesterov(dense_sum / groups, anchor_dense, momentum_dense)
    weights = lax.all_gather(dense_new.astype(bf16), "shard", axis=0, tiled=True)
    across = functools.partial(
        lax.dot_general,
        dimension_numbers=(((0,), (0,)), ((), ())),
        precision=highest,
        preferred_element_type=f32,
    )
    gram = lax.psum(across(factor, factor), "shard")
    chol = jnp.linalg.cholesky(gram)
    ortho = jax.scipy.linalg.solve_triangular(chol, factor.T, lower=True).T
    share = lax.psum_scatter(across(diff, ortho), "shard", scatter_dimension=0, tiled=True)
    coeff = lax.all_gather(lax.psum(share, "rep"), "shard", axis=0, tiled=True)
    grad = (
        lax.dot_general(ortho, coeff, (((1,), (1,)), ((), ())), precision=highest, preferred_element_type=f32)
        / groups
    )
    emb_new, emb_mom = nesterov(grad, anchor_emb, momentum_emb)
    return (dense_new, dense_mom, weights, emb_new, emb_mom)


GROUPS = 4
CORES = 2
CHUNKS = GROUPS * CORES
N_COPIES = 48


def exchange_kernel(
    local_hbm, anchor_hbm, ld_ref, ad_ref, md_ref, basis_ref,
    h_ref, x_ref, dg_ref, dw_ref,
    lbuf, abuf, eh, el, bas, dd, drecv, f2, frecv, fsum, xt_ref, m_ref, mrecv1, mrecv2, msum, mrecv3, mz,
    gsend, grecv, gz, gram,
    lsem, asem, ssem, rsem,
):
    rep = lax.axis_index("rep")
    shard = lax.axis_index("shard")
    z, core = shard // CORES, shard % CORES
    other = 1 - core
    width = lbuf.shape[2]
    rank = basis_ref.shape[1]

    def rep_dev(j):
        return ((rep + j) % GROUPS, shard)

    def z_dev(j):
        return (rep, ((z + j) % GROUPS) * CORES + core)

    core_dev = (rep, z * CORES + other)
    started = []

    def send(src, dst, dev):
        i = len(started)
        copy = pltpu.make_async_remote_copy(
            src_ref=src, dst_ref=dst, send_sem=ssem.at[i], recv_sem=rsem.at[i],
            device_id=dev, device_id_type=MESH,
        )
        copy.start()
        started.append(copy)
        return copy

    def load(k, start):
        cols = pl.ds(pl.multiple_of(k * width, width), width)
        for src, dst, sem in ((local_hbm, lbuf, lsem), (anchor_hbm, abuf, asem)):
            copy = pltpu.make_async_copy(src.at[:, cols], dst.at[k], sem.at[k])
            if start:
                copy.start()
            else:
                copy.wait()

    @pl.loop(0, CHUNKS)
    def _(k):
        load(k, True)

    barrier = pltpu.get_barrier_semaphore()
    peers = [core_dev] + [rep_dev(j) for j in (1, 2, 3)] + [z_dev(j) for j in (1, 2, 3)]
    for dev in peers:
        pl.semaphore_signal(barrier, inc=1, device_id=dev, device_id_type=MESH)

    b = basis_ref[...]
    b_hi = b.astype(bf16)
    b_lo = (b - b_hi.astype(f32)).astype(bf16)
    bas[shard] = jnp.concatenate([b_hi, b_lo], axis=1)
    dd[...] = ad_ref[...] - ld_ref[...]
    pl.semaphore_wait(barrier, len(peers))

    basis_z = [send(bas.at[shard], bas.at[shard], z_dev(j)) for j in (1, 2, 3)]
    basis_core = [send(bas.at[shard], bas.at[shard], core_dev)]
    dense_rs = [send(dd.at[(rep + j) % GROUPS], drecv.at[j - 1], rep_dev(j)) for j in (1, 2, 3)]

    def split(k):
        load(k, False)
        e = abuf[k] - lbuf[k]
        hi = e.astype(bf16)
        eh[k] = hi
        el[k] = (e - hi.astype(f32)).astype(bf16)

    pl.loop(0, CHUNKS - 2)(split)
    for j in (1, 2, 3):
        basis_z[j - 1].wait_recv()
        at = ((z + GROUPS - j) % GROUPS) * CORES + core
        basis_core.append(send(bas.at[at], bas.at[at], core_dev))
    pl.loop(CHUNKS - 2, CHUNKS)(split)
    for copy in basis_core:
        copy.wait_recv()

    half = f2.shape[0] * f2.shape[1]
    lanes = f2.shape[2]
    piece = f2.shape[1]

    @pl.loop(0, GROUPS)
    def _(q):
        def summed(start):
            rows = pl.ds(pl.multiple_of(start + q * piece, piece), piece)
            total = jnp.zeros((piece, lanes), f32)
            for k in range(CHUNKS):
                total += jnp.dot(eh[k, rows, :], bas[k], preferred_element_type=f32)
                total += jnp.dot(el[k, rows, :], bas[k], preferred_element_type=f32)
            return total + pltpu.roll(total, rank, 1)

        lane = lax.broadcasted_iota(jnp.int32, (piece, lanes), 1)
        f2[q] = jnp.where(lane < rank, summed(0), summed(half))

    factor_rs = [send(f2.at[(rep + j) % GROUPS], frecv.at[j - 1], rep_dev(j)) for j in (1, 2, 3)]

    for copy in dense_rs:
        copy.wait_recv()
    dg_ref[rep] = (dd[rep] + drecv[0] + drecv[1] + drecv[2]) / GROUPS
    new_dense, _ = nesterov(dg_ref[rep], ad_ref[rep], md_ref[rep])
    dw_ref[core, rep, z] = new_dense.astype(bf16)

    for copy in factor_rs:
        copy.wait_recv()
    fsum[rep] = f2[rep] + frecv[0] + frecv[1] + frecv[2]
    factor_ag = [send(fsum.at[rep], fsum.at[rep], rep_dev(j)) for j in (1, 2, 3)]
    dense_ag = [send(dg_ref.at[rep], dg_ref.at[rep], rep_dev(j)) for j in (1, 2, 3)]
    mine = dw_ref.at[core, rep, z]
    weights_z = [send(mine, mine, z_dev(j)) for j in (1, 2, 3)]
    for copy in factor_ag:
        copy.wait_recv()

    lane = lax.broadcasted_iota(jnp.int32, (piece, lanes), 1)
    for q in range(GROUPS):
        here = fsum[q]
        there = pltpu.roll(here, rank, 1)
        for top, twice in ((0, jnp.where(lane < rank, here, there)), (half, jnp.where(lane < rank, there, here))):
            hi = twice.astype(bf16).astype(f32)
            x = jnp.where(lane < rank, hi, twice - hi)
            at = top + q * piece
            x_ref[at : at + piece, :] = x.astype(bf16)
            xt_ref[:, at : at + piece] = x.T.astype(bf16)

    g = jnp.dot(xt_ref[...], x_ref[...], preferred_element_type=f32)
    g = g[:rank] + g[rank:]
    g = g + pltpu.roll(g, rank, 1)
    fold = rank // 2
    lane_g = lax.broadcasted_iota(jnp.int32, (fold, lanes), 1)
    gsend[...] = jnp.where(lane_g < rank, g[:fold], g[fold:])
    gram_core = send(gsend, grecv, core_dev)

    @pl.loop(0, CHUNKS)
    def _(k):
        m = jnp.dot(xt_ref[...], eh[k], preferred_element_type=f32)
        m += jnp.dot(xt_ref[...], el[k], preferred_element_type=f32)
        m_ref[k] = m[:rank] + m[rank:]

    coeff_core = send(m_ref.at[pl.ds(other * GROUPS, GROUPS)], mrecv1, core_dev)
    gram_core.wait_recv()
    gz[z] = gsend[...] + grecv[...]
    gram_z = [send(gz.at[z], gz.at[z], z_dev(j)) for j in (1, 2, 3)]

    coeff_core.wait_recv()
    mrecv1[...] += m_ref[pl.ds(core * GROUPS, GROUPS)]
    coeff_rs = [send(mrecv1.at[(rep + j) % GROUPS], mrecv2.at[j - 1], rep_dev(j)) for j in (1, 2, 3)]

    for copy in weights_z:
        copy.wait_recv()
    ours = dw_ref.at[core, rep]
    weights_rep = [send(ours, ours, rep_dev(j)) for j in (1, 2, 3)]

    for copy in gram_z:
        copy.wait_recv()
    folded = gz[0] + gz[1] + gz[2] + gz[3]
    back = pltpu.roll(folded, rank, 1)
    gram[:fold] = folded
    gram[fold:] = back

    sub_i = lax.broadcasted_iota(jnp.int32, (rank, lanes), 0)
    lane_i = lax.broadcasted_iota(jnp.int32, (rank, lanes), 1)
    lane_1 = lax.broadcasted_iota(jnp.int32, (1, lanes), 1)

    @pl.loop(0, rank)
    def _(k):
        a = gram[...]
        row = gram[pl.ds(k, 1), :]
        at_k = lane_i == k
        col = jnp.sum(jnp.where(at_k, a, 0.0), axis=1, keepdims=True)
        pivot = jnp.sum(jnp.where(lane_1 == k, row, 0.0), axis=1, keepdims=True)
        scaled = jnp.where(lane_1 == k, 1.0, row) / pivot
        gram[...] = jnp.where(sub_i == k, scaled, jnp.where(at_k, 0.0, a) - col * scaled)

    for copy in coeff_rs:
        copy.wait_recv()
    msum[...] = (mrecv1[rep] + mrecv2[0] + mrecv2[1] + mrecv2[2]).reshape(msum.shape)
    coeff_z = [send(msum.at[(z + j) % GROUPS], mrecv3.at[j - 1], z_dev(j)) for j in (1, 2, 3)]
    for copy in coeff_z:
        copy.wait_recv()
    mz[z] = msum[z] + mrecv3[0] + mrecv3[1] + mrecv3[2]
    coeff_zag = [send(mz.at[z], mz.at[z], z_dev(j)) for j in (1, 2, 3)]
    for copy in coeff_zag:
        copy.wait_recv()
    h = jnp.dot(gram[:, :rank], mz[...].reshape(rank, width), precision=highest, preferred_element_type=f32)
    h = h / GROUPS
    h_hi = h.astype(bf16)
    own = core * GROUPS + rep
    h_ref[own, :rank, :] = h_hi
    h_ref[own, rank:, :] = (h - h_hi.astype(f32)).astype(bf16)
    h_rep = [send(h_ref.at[own], h_ref.at[own], rep_dev(j)) for j in (1, 2, 3)]
    h_core = [send(h_ref.at[own], h_ref.at[own], core_dev)]
    for j in (1, 2, 3):
        h_rep[j - 1].wait_recv()
        at = core * GROUPS + (rep + GROUPS - j) % GROUPS
        h_core.append(send(h_ref.at[at], h_ref.at[at], core_dev))

    for copy in weights_rep:
        copy.wait_recv()
    weights_core = send(dw_ref.at[core], dw_ref.at[core], core_dev)
    for copy in dense_ag + h_core + [weights_core]:
        copy.wait_recv()
    for copy in started:
        copy.wait_send()


def update_kernel(x_ref, h_ref, anchor_ref, mom_ref, dg_ref, ad_ref, md_ref, dw_ref,
                  dn_out, dm_out, dw_out, new_out, mom_out):
    x = x_ref[...]
    rank = h_ref.shape[1] // 2
    width = h_ref.shape[2]
    x2 = jnp.concatenate([x, x], axis=1)
    for k in range(h_ref.shape[0]):
        cols = slice(k * width, (k + 1) * width)
        hi, lo = h_ref[k, :rank, :], h_ref[k, rank:, :]
        grad = jnp.dot(x2, jnp.concatenate([hi, hi, lo, lo], axis=0), preferred_element_type=f32)
        new_out[:, cols], mom_out[:, cols] = nesterov(grad, anchor_ref[:, cols], mom_ref[:, cols])
    dn_out[...], dm_out[...] = nesterov(dg_ref[...], ad_ref[...], md_ref[...])
    dw_out[...] = dw_ref[...].reshape(dw_out.shape)


def fused(local_dense, anchor_dense, momentum_dense, local_emb, anchor_emb, momentum_emb, proj_basis):
    rows, cols = anchor_emb.shape
    drows, dcols = anchor_dense.shape
    rank = proj_basis.shape[1]
    width = cols // CHUNKS
    dq = drows // GROUPS
    piece = rows // 2 // GROUPS
    lanes = 2 * rank
    quarters = (GROUPS, dq, dcols)
    vmem = pl.BlockSpec(memory_space=pltpu.VMEM)
    hbm = pl.BlockSpec(memory_space=pltpu.HBM)
    S = jax.ShapeDtypeStruct
    h, x, dg, dw = pl.pallas_call(
        exchange_kernel,
        out_shape=(
            S((CHUNKS, lanes, width), bf16),
            S((rows, lanes), bf16),
            S(quarters, f32),
            S((CORES, GROUPS, GROUPS, dq, dcols), bf16),
        ),
        in_specs=[hbm, hbm] + [vmem] * 4,
        out_specs=(vmem,) * 4,
        scratch_shapes=[
            pltpu.VMEM((CHUNKS, rows, width), f32),
            pltpu.VMEM((CHUNKS, rows, width), f32),
            pltpu.VMEM((CHUNKS, rows, width), bf16),
            pltpu.VMEM((CHUNKS, rows, width), bf16),
            pltpu.VMEM((CHUNKS, width, lanes), bf16),
            pltpu.VMEM(quarters, f32),
            pltpu.VMEM((3, dq, dcols), f32),
            pltpu.VMEM((GROUPS, piece, lanes), f32),
            pltpu.VMEM((3, piece, lanes), f32),
            pltpu.VMEM((GROUPS, piece, lanes), f32),
            pltpu.VMEM((lanes, rows), bf16),
            pltpu.VMEM((CHUNKS, rank, width), f32),
            pltpu.VMEM((GROUPS, rank, width), f32),
            pltpu.VMEM((3, rank, width), f32),
            pltpu.VMEM((GROUPS, rank // GROUPS, width), f32),
            pltpu.VMEM((3, rank // GROUPS, width), f32),
            pltpu.VMEM((GROUPS, rank // GROUPS, width), f32),
            pltpu.VMEM((rank // 2, lanes), f32),
            pltpu.VMEM((rank // 2, lanes), f32),
            pltpu.VMEM((GROUPS, rank // 2, lanes), f32),
            pltpu.VMEM((rank, lanes), f32),
            pltpu.SemaphoreType.DMA((CHUNKS,)),
            pltpu.SemaphoreType.DMA((CHUNKS,)),
            pltpu.SemaphoreType.DMA((N_COPIES,)),
            pltpu.SemaphoreType.DMA((N_COPIES,)),
        ],
        compiler_params=pltpu.CompilerParams(
            collective_id=0, has_side_effects=True, vmem_limit_bytes=52 * 1024 * 1024
        ),
    )(
        local_emb[0], anchor_emb, local_dense[0].reshape(quarters), anchor_dense.reshape(quarters),
        momentum_dense.reshape(quarters), proj_basis,
    )

    steps = CHUNKS
    block = (rows // steps, cols)
    dense_block = (drows // steps, dcols)
    by_row = lambda shape: pl.BlockSpec(shape, lambda i: (i, 0))
    return pl.pallas_call(
        update_kernel,
        grid=(steps,),
        out_shape=(
            S(anchor_dense.shape, f32),
            S(anchor_dense.shape, f32),
            S((drows * CHUNKS, dcols), bf16),
            S(anchor_emb.shape, f32),
            S(anchor_emb.shape, f32),
        ),
        in_specs=[
            by_row((rows // steps, lanes)),
            pl.BlockSpec((CHUNKS, lanes, width), lambda i: (0, 0, 0)),
            by_row(block),
            by_row(block),
            by_row(dense_block),
            by_row(dense_block),
            by_row(dense_block),
            pl.BlockSpec((1, GROUPS, 1, dq, dcols), lambda i: (i % CORES, 0, i // CORES, 0, 0)),
        ],
        out_specs=(
            by_row(dense_block),
            by_row(dense_block),
            by_row((drows, dcols)),
            by_row(block),
            by_row(block),
        ),
        compiler_params=pltpu.CompilerParams(vmem_limit_bytes=40 * 1024 * 1024),
    )(x, h, anchor_emb, momentum_emb, dg.reshape(anchor_dense.shape), anchor_dense, momentum_dense, dw)


def solution(mesh):
    fits = mesh.shape["rep"] == GROUPS and mesh.shape["shard"] == CHUNKS
    placed = (
        P("rep", "shard", None),
        P("shard", None),
        P("shard", None),
        P("rep", "shard", None),
        P("shard", None),
        P("shard", None),
        P("shard", None),
    )
    return jax.shard_map(
        fused if fits else plain,
        mesh=mesh,
        in_specs=placed,
        out_specs=(P("shard", None), P("shard", None), P(), P("shard", None), P("shard", None)),
        check_vma=False,
    )
```

```python
import functools

import jax
import jax.numpy as jnp
from jax import lax
from jax.experimental import pallas as pl
from jax.experimental.pallas import tpu as pltpu
from jax.sharding import PartitionSpec as P

outer_rate = 0.7
momentum_rate = 0.9
highest = lax.Precision.HIGHEST
f32 = jnp.float32
bf16 = jnp.bfloat16
MESH = pl.DeviceIdType.MESH


def nesterov(grad, anchor, momentum):
    mom = momentum_rate * momentum + grad
    return anchor - outer_rate * (grad + momentum_rate * mom), mom


def plain(local_dense, anchor_dense, momentum_dense, local_emb, anchor_emb, momentum_emb, proj_basis):
    groups = lax.axis_size("rep")
    basis = lax.all_gather(proj_basis, "shard", axis=0, tiled=True)
    diff = anchor_emb - local_emb[0]
    part = jnp.dot(diff, basis, precision=highest, preferred_element_type=f32)
    dense_sum, factor = lax.psum((anchor_dense - local_dense[0], part), "rep")
    dense_new, dense_mom = nesterov(dense_sum / groups, anchor_dense, momentum_dense)
    weights = lax.all_gather(dense_new.astype(bf16), "shard", axis=0, tiled=True)
    across = functools.partial(
        lax.dot_general,
        dimension_numbers=(((0,), (0,)), ((), ())),
        precision=highest,
        preferred_element_type=f32,
    )
    gram = lax.psum(across(factor, factor), "shard")
    chol = jnp.linalg.cholesky(gram)
    ortho = jax.scipy.linalg.solve_triangular(chol, factor.T, lower=True).T
    share = lax.psum_scatter(across(diff, ortho), "shard", scatter_dimension=0, tiled=True)
    coeff = lax.all_gather(lax.psum(share, "rep"), "shard", axis=0, tiled=True)
    grad = (
        lax.dot_general(ortho, coeff, (((1,), (1,)), ((), ())), precision=highest, preferred_element_type=f32)
        / groups
    )
    emb_new, emb_mom = nesterov(grad, anchor_emb, momentum_emb)
    return (dense_new, dense_mom, weights, emb_new, emb_mom)


GROUPS = 4
CORES = 2
CHUNKS = GROUPS * CORES
N_COPIES = 64
LIMIT1 = 28 * 1024 * 1024
LIMIT2 = 28 * 1024 * 1024


def exchange_kernel(
    local_hbm, anchor_hbm, momentum_hbm, ld_ref, ad_ref, md_ref, basis_ref,
    h_ref, x_ref, dg_ref, dw_ref, abuf, mbuf,
    lbuf, eh, el, bas, dd, drecv, f2, frecv, fsum, xt_ref, m_ref, mrecv1, mrecv2, msum, mrecv3, mz,
    gsend, grecv, gz, gram,
    lsem, asem, msem, ssem, rsem,
):
    rep = lax.axis_index("rep")
    shard = lax.axis_index("shard")
    z, core = shard // CORES, shard % CORES
    other = 1 - core
    width = lbuf.shape[2]
    rank = basis_ref.shape[1]

    def rep_dev(j):
        return ((rep + j) % GROUPS, shard)

    def z_dev(j):
        return (rep, ((z + j) % GROUPS) * CORES + core)

    core_dev = (rep, z * CORES + other)
    started = []

    def send(src, dst, dev):
        i = len(started)
        copy = pltpu.make_async_remote_copy(
            src_ref=src, dst_ref=dst, send_sem=ssem.at[i], recv_sem=rsem.at[i],
            device_id=dev, device_id_type=MESH,
        )
        copy.start()
        started.append(copy)
        return copy

    differences = ((local_hbm, lbuf, lsem), (anchor_hbm, abuf, asem))
    momenta = ((momentum_hbm, mbuf, msem),)

    def load(k, start, arrays=differences):
        cols = pl.ds(pl.multiple_of(k * width, width), width)
        for src, dst, sem in arrays:
            copy = pltpu.make_async_copy(src.at[:, cols], dst.at[k], sem.at[k])
            if start:
                copy.start()
            else:
                copy.wait()

    @pl.loop(0, CHUNKS)
    def _(k):
        load(k, True)

    barrier = pltpu.get_barrier_semaphore()
    peers = [core_dev] + [rep_dev(j) for j in (1, 2, 3)] + [z_dev(j) for j in (1, 2, 3)]
    for dev in peers:
        pl.semaphore_signal(barrier, inc=1, device_id=dev, device_id_type=MESH)

    b = basis_ref[...]
    b_hi = b.astype(bf16)
    b_lo = (b - b_hi.astype(f32)).astype(bf16)
    bas[shard] = jnp.concatenate([b_hi, b_lo], axis=1)
    dd[...] = ad_ref[...] - ld_ref[...]
    pl.semaphore_wait(barrier, len(peers))

    basis_z = [send(bas.at[shard], bas.at[shard], z_dev(j)) for j in (1, 2, 3)]
    basis_core = [send(bas.at[shard], bas.at[shard], core_dev)]
    dense_rs = [send(dd.at[(rep + j) % GROUPS], drecv.at[j - 1], rep_dev(j)) for j in (1, 2, 3)]

    def split(k):
        load(k, False)
        e = abuf[k] - lbuf[k]
        hi = e.astype(bf16)
        eh[k] = hi
        el[k] = (e - hi.astype(f32)).astype(bf16)

    pl.loop(0, CHUNKS - 2)(split)
    for j in (1, 2, 3):
        basis_z[j - 1].wait_recv()
        at = ((z + GROUPS - j) % GROUPS) * CORES + core
        basis_core.append(send(bas.at[at], bas.at[at], core_dev))
    pl.loop(CHUNKS - 2, CHUNKS)(split)

    @pl.loop(0, CHUNKS)
    def _(k):
        load(k, True, momenta)

    for copy in basis_core:
        copy.wait_recv()

    half = f2.shape[0] * f2.shape[1]
    lanes = f2.shape[2]
    piece = f2.shape[1]

    def summed(start):
        total = jnp.zeros((half, lanes), f32)
        for k in range(CHUNKS):
            total += jnp.dot(eh[k, start : start + half, :], bas[k], preferred_element_type=f32)
            total += jnp.dot(el[k, start : start + half, :], bas[k], preferred_element_type=f32)
        return total + pltpu.roll(total, rank, 1)

    lane_f = lax.broadcasted_iota(jnp.int32, (half, lanes), 1)
    f2[...] = jnp.where(lane_f < rank, summed(0), summed(half)).reshape(f2.shape)

    factor_rs = [send(f2.at[(rep + j) % GROUPS], frecv.at[j - 1], rep_dev(j)) for j in (1, 2, 3)]

    for copy in dense_rs:
        copy.wait_recv()
    dg_ref[rep] = (dd[rep] + drecv[0] + drecv[1] + drecv[2]) / GROUPS
    new_dense, _ = nesterov(dg_ref[rep], ad_ref[rep], md_ref[rep])
    dw_ref[core, rep, z] = new_dense.astype(bf16)

    for copy in factor_rs:
        copy.wait_recv()
    fsum[rep] = f2[rep] + frecv[0] + frecv[1] + frecv[2]
    factor_ag = [send(fsum.at[rep], fsum.at[rep], rep_dev(j)) for j in (1, 2, 3)]
    dense_ag = [send(dg_ref.at[rep], dg_ref.at[rep], rep_dev(j)) for j in (1, 2, 3)]
    mine = dw_ref.at[core, rep, z]
    weights_z = [send(mine, mine, z_dev(j)) for j in (1, 2, 3)]
    for copy in factor_ag:
        copy.wait_recv()

    lane = lax.broadcasted_iota(jnp.int32, (piece, lanes), 1)
    for q in range(GROUPS):
        here = fsum[q]
        there = pltpu.roll(here, rank, 1)
        for top, twice in ((0, jnp.where(lane < rank, here, there)), (half, jnp.where(lane < rank, there, here))):
            hi = twice.astype(bf16).astype(f32)
            x = jnp.where(lane < rank, hi, twice - hi)
            at = top + q * piece
            x_ref[at : at + piece, :] = x.astype(bf16)
            xt_ref[:, at : at + piece] = x.T.astype(bf16)

    g = jnp.dot(xt_ref[...], x_ref[...], preferred_element_type=f32)
    g = g[:rank] + g[rank:]
    g = g + pltpu.roll(g, rank, 1)
    fold = rank // 2
    lane_g = lax.broadcasted_iota(jnp.int32, (fold, lanes), 1)
    gsend[...] = jnp.where(lane_g < rank, g[:fold], g[fold:])
    gram_core = send(gsend, grecv, core_dev)

    for copy in weights_z:
        copy.wait_recv()
    first, second = pl.ds(0, GROUPS // 2), pl.ds(GROUPS // 2, GROUPS // 2)
    ours = dw_ref.at[core, rep, first]
    weights_first = [send(ours, ours, rep_dev(j)) for j in (1, 2, 3)]

    @pl.loop(0, CHUNKS)
    def _(k):
        m = jnp.dot(xt_ref[...], eh[k], preferred_element_type=f32)
        m += jnp.dot(xt_ref[...], el[k], preferred_element_type=f32)
        m_ref[k] = m[:rank] + m[rank:]

    coeff_core = send(m_ref.at[pl.ds(other * GROUPS, GROUPS)], mrecv1, core_dev)
    gram_core.wait_recv()
    gz[z] = gsend[...] + grecv[...]
    gram_z = [send(gz.at[z], gz.at[z], z_dev(j)) for j in (1, 2, 3)]

    coeff_core.wait_recv()
    mrecv1[...] += m_ref[pl.ds(core * GROUPS, GROUPS)]
    coeff_rs = [send(mrecv1.at[(rep + j) % GROUPS], mrecv2.at[j - 1], rep_dev(j)) for j in (1, 2, 3)]

    ours = dw_ref.at[core, rep, second]
    weights_second = [send(ours, ours, rep_dev(j)) for j in (1, 2, 3)]

    for copy in gram_z:
        copy.wait_recv()
    folded = gz[0] + gz[1] + gz[2] + gz[3]
    back = pltpu.roll(folded, rank, 1)
    gram[:fold] = folded
    gram[fold:] = back

    sub_i = lax.broadcasted_iota(jnp.int32, (rank, lanes), 0)
    lane_i = lax.broadcasted_iota(jnp.int32, (rank, lanes), 1)
    lane_1 = lax.broadcasted_iota(jnp.int32, (1, lanes), 1)

    def pick(values, at):
        return jnp.sum(jnp.where(at, values, 0.0), axis=1, keepdims=True)

    def eliminate_two(pair):
        k = pair * 2
        a = gram[...]
        row0, row1 = gram[pl.ds(k, 1), :], gram[pl.ds(k + 1, 1), :]
        at0, at1 = lane_i == k, lane_i == k + 1
        one0, one1 = lane_1 == k, lane_1 == k + 1
        col0, col1 = pick(a, at0), pick(a, at1)
        s00, s01, s10, s11 = pick(row0, one0), pick(row0, one1), pick(row1, one0), pick(row1, one1)
        p0 = jnp.where(one0, 1.0, row0) / s00
        q01 = s01 / s00
        row1 = jnp.where(one0, 0.0, row1) - s10 * p0
        p1 = jnp.where(one1, 1.0, row1) / (s11 - s10 * q01)
        p0 = jnp.where(one1, 0.0, p0)
        col1 = col1 - col0 * q01
        rest = jnp.where(at0 | at1, 0.0, a) - col0 * p0 - col1 * p1
        gram[...] = jnp.where(sub_i == k, p0 - q01 * p1, jnp.where(sub_i == k + 1, p1, rest))

    pl.loop(0, rank // 4)(eliminate_two)
    for copy in coeff_rs:
        copy.wait_recv()
    msum[...] = (mrecv1[rep] + mrecv2[0] + mrecv2[1] + mrecv2[2]).reshape(msum.shape)
    coeff_z = [send(msum.at[(z + j) % GROUPS], mrecv3.at[j - 1], z_dev(j)) for j in (1, 2, 3)]
    pl.loop(rank // 4, 3 * rank // 8)(eliminate_two)
    for copy in coeff_z:
        copy.wait_recv()
    mz[z] = msum[z] + mrecv3[0] + mrecv3[1] + mrecv3[2]
    coeff_zag = [send(mz.at[z], mz.at[z], z_dev(j)) for j in (1, 2, 3)]
    pl.loop(3 * rank // 8, rank // 2)(eliminate_two)
    for copy in coeff_zag:
        copy.wait_recv()
    h = jnp.dot(gram[:, :rank], mz[...].reshape(rank, width), precision=highest, preferred_element_type=f32)
    h = h / GROUPS
    h_hi = h.astype(bf16)
    own = core * GROUPS + rep
    h_ref[own, :rank, :] = h_hi
    h_ref[own, rank:, :] = (h - h_hi.astype(f32)).astype(bf16)
    h_rep = [send(h_ref.at[own], h_ref.at[own], rep_dev(j)) for j in (1, 2, 3)]
    h_core = [send(h_ref.at[own], h_ref.at[own], core_dev)]
    for j in (1, 2, 3):
        h_rep[j - 1].wait_recv()
        at = core * GROUPS + (rep + GROUPS - j) % GROUPS
        h_core.append(send(h_ref.at[at], h_ref.at[at], core_dev))

    weights_core = []
    for part, arrivals in ((first, weights_first), (second, weights_second)):
        for copy in arrivals:
            copy.wait_recv()
        here = dw_ref.at[core, :, part]
        weights_core.append(send(here, here, core_dev))
    for copy in dense_ag + h_core + weights_core:
        copy.wait_recv()

    @pl.loop(0, CHUNKS)
    def _(k):
        load(k, False, momenta)

    for copy in started:
        copy.wait_send()


def update_kernel(x_ref, h_ref, anchor_ref, mom_ref, dg_ref, ad_ref, md_ref, dw_ref,
                  dn_out, dm_out, dw_out, new_out, mom_out, nbuf, pbuf, nsem, psem, wsem):
    rank = h_ref.shape[1] // 2
    width = h_ref.shape[2]
    rows = x_ref.shape[0]
    step = rows // 4

    def weights(at):
        return pltpu.make_async_copy(
            dw_ref.at[at % CORES, :, at // CORES], dw_out.at[at // CORES, at % CORES], wsem.at[at]
        )

    def out(k):
        cols = pl.ds(k * width, width)
        return (
            pltpu.make_async_copy(nbuf.at[k % 2], new_out.at[:, cols], nsem.at[k % 2]),
            pltpu.make_async_copy(pbuf.at[k % 2], mom_out.at[:, cols], psem.at[k % 2]),
        )

    for at in range(CHUNKS):
        weights(at).start()
    for k in range(CHUNKS):
        hi, lo = h_ref[k, :rank, :], h_ref[k, rank:, :]
        right = jnp.concatenate([hi, hi, lo, lo], axis=0)
        if k >= 2:
            for copy in out(k - 2):
                copy.wait()

        @pl.loop(0, rows // step)
        def _(t):
            at = pl.ds(pl.multiple_of(t * step, step), step)
            x = x_ref[at, :]
            grad = jnp.dot(jnp.concatenate([x, x], axis=1), right, preferred_element_type=f32)
            nbuf[k % 2, at, :], pbuf[k % 2, at, :] = nesterov(grad, anchor_ref[k, at, :], mom_ref[k, at, :])

        for copy in out(k):
            copy.start()
    dn_out[...], dm_out[...] = nesterov(dg_ref[...], ad_ref[...], md_ref[...])
    for k in (CHUNKS - 2, CHUNKS - 1):
        for copy in out(k):
            copy.wait()
    for at in range(CHUNKS):
        weights(at).wait()


def fused(local_dense, anchor_dense, momentum_dense, local_emb, anchor_emb, momentum_emb, proj_basis):
    rows, cols = anchor_emb.shape
    drows, dcols = anchor_dense.shape
    rank = proj_basis.shape[1]
    width = cols // CHUNKS
    dq = drows // GROUPS
    piece = rows // 2 // GROUPS
    lanes = 2 * rank
    quarters = (GROUPS, dq, dcols)
    vmem = pl.BlockSpec(memory_space=pltpu.VMEM)
    hbm = pl.BlockSpec(memory_space=pltpu.HBM)
    S = jax.ShapeDtypeStruct
    h, x, dg, dw, anchor, momentum = pl.pallas_call(
        exchange_kernel,
        out_shape=(
            S((CHUNKS, lanes, width), bf16),
            S((rows, lanes), bf16),
            S(quarters, f32),
            S((CORES, GROUPS, GROUPS, dq, dcols), bf16),
            S((CHUNKS, rows, width), f32),
            S((CHUNKS, rows, width), f32),
        ),
        in_specs=[hbm] * 3 + [vmem] * 4,
        out_specs=(vmem,) * 6,
        scratch_shapes=[
            pltpu.VMEM((CHUNKS, rows, width), f32),
            pltpu.VMEM((CHUNKS, rows, width), bf16),
            pltpu.VMEM((CHUNKS, rows, width), bf16),
            pltpu.VMEM((CHUNKS, width, lanes), bf16),
            pltpu.VMEM(quarters, f32),
            pltpu.VMEM((3, dq, dcols), f32),
            pltpu.VMEM((GROUPS, piece, lanes), f32),
            pltpu.VMEM((3, piece, lanes), f32),
            pltpu.VMEM((GROUPS, piece, lanes), f32),
            pltpu.VMEM((lanes, rows), bf16),
            pltpu.VMEM((CHUNKS, rank, width), f32),
            pltpu.VMEM((GROUPS, rank, width), f32),
            pltpu.VMEM((3, rank, width), f32),
            pltpu.VMEM((GROUPS, rank // GROUPS, width), f32),
            pltpu.VMEM((3, rank // GROUPS, width), f32),
            pltpu.VMEM((GROUPS, rank // GROUPS, width), f32),
            pltpu.VMEM((rank // 2, lanes), f32),
            pltpu.VMEM((rank // 2, lanes), f32),
            pltpu.VMEM((GROUPS, rank // 2, lanes), f32),
            pltpu.VMEM((rank, lanes), f32),
            pltpu.SemaphoreType.DMA((CHUNKS,)),
            pltpu.SemaphoreType.DMA((CHUNKS,)),
            pltpu.SemaphoreType.DMA((CHUNKS,)),
            pltpu.SemaphoreType.DMA((N_COPIES,)),
            pltpu.SemaphoreType.DMA((N_COPIES,)),
        ],
        compiler_params=pltpu.CompilerParams(
            collective_id=0, has_side_effects=True, vmem_limit_bytes=LIMIT1
        ),
    )(
        local_emb[0], anchor_emb, momentum_emb, local_dense[0].reshape(quarters), anchor_dense.reshape(quarters),
        momentum_dense.reshape(quarters), proj_basis,
    )

    dn, dm, weights, new, mom = pl.pallas_call(
        update_kernel,
        out_shape=(
            S(anchor_dense.shape, f32),
            S(anchor_dense.shape, f32),
            S((GROUPS, CORES, GROUPS, dq, dcols), bf16),
            S(anchor_emb.shape, f32),
            S(anchor_emb.shape, f32),
        ),
        in_specs=[vmem] * 8,
        out_specs=(vmem, vmem, hbm, hbm, hbm),
        scratch_shapes=[
            pltpu.VMEM((2, rows, width), f32),
            pltpu.VMEM((2, rows, width), f32),
            pltpu.SemaphoreType.DMA((2,)),
            pltpu.SemaphoreType.DMA((2,)),
            pltpu.SemaphoreType.DMA((CHUNKS,)),
        ],
        compiler_params=pltpu.CompilerParams(vmem_limit_bytes=LIMIT2),
    )(x, h, anchor, momentum, dg.reshape(anchor_dense.shape), anchor_dense, momentum_dense, dw)
    return dn, dm, weights.reshape(drows * CHUNKS, dcols), new, mom


def solution(mesh):
    fits = mesh.shape["rep"] == GROUPS and mesh.shape["shard"] == CHUNKS
    placed = (
        P("rep", "shard", None),
        P("shard", None),
        P("shard", None),
        P("rep", "shard", None),
        P("shard", None),
        P("shard", None),
        P("shard", None),
    )
    return jax.shard_map(
        fused if fits else plain,
        mesh=mesh,
        in_specs=placed,
        out_specs=(P("shard", None), P("shard", None), P(), P("shard", None), P("shard", None)),
        check_vma=False,
    )
```

```python
import functools

import jax
import jax.numpy as jnp
from jax import lax
from jax.experimental import pallas as pl
from jax.experimental.pallas import tpu as pltpu
from jax.sharding import PartitionSpec as P

outer_rate = 0.7
momentum_rate = 0.9
highest = lax.Precision.HIGHEST
f32 = jnp.float32
bf16 = jnp.bfloat16
MESH = pl.DeviceIdType.MESH


def nesterov(grad, anchor, momentum):
    mom = momentum_rate * momentum + grad
    return anchor - outer_rate * (grad + momentum_rate * mom), mom


def plain(local_dense, anchor_dense, momentum_dense, local_emb, anchor_emb, momentum_emb, proj_basis):
    groups = lax.axis_size("rep")
    basis = lax.all_gather(proj_basis, "shard", axis=0, tiled=True)
    diff = anchor_emb - local_emb[0]
    part = jnp.dot(diff, basis, precision=highest, preferred_element_type=f32)
    dense_sum, factor = lax.psum((anchor_dense - local_dense[0], part), "rep")
    dense_new, dense_mom = nesterov(dense_sum / groups, anchor_dense, momentum_dense)
    weights = lax.all_gather(dense_new.astype(bf16), "shard", axis=0, tiled=True)
    across = functools.partial(
        lax.dot_general,
        dimension_numbers=(((0,), (0,)), ((), ())),
        precision=highest,
        preferred_element_type=f32,
    )
    gram = lax.psum(across(factor, factor), "shard")
    chol = jnp.linalg.cholesky(gram)
    ortho = jax.scipy.linalg.solve_triangular(chol, factor.T, lower=True).T
    share = lax.psum_scatter(across(diff, ortho), "shard", scatter_dimension=0, tiled=True)
    coeff = lax.all_gather(lax.psum(share, "rep"), "shard", axis=0, tiled=True)
    grad = (
        lax.dot_general(ortho, coeff, (((1,), (1,)), ((), ())), precision=highest, preferred_element_type=f32)
        / groups
    )
    emb_new, emb_mom = nesterov(grad, anchor_emb, momentum_emb)
    return (dense_new, dense_mom, weights, emb_new, emb_mom)


GROUPS = 4
CORES = 2
CHUNKS = GROUPS * CORES
N_COPIES = 64
LIMIT1 = 28 * 1024 * 1024
LIMIT2 = 28 * 1024 * 1024


def exchange_kernel(
    local_hbm, anchor_hbm, momentum_hbm, ld_hbm, ad_hbm, md_hbm, basis_hbm,
    h_ref, x_ref, dg_ref, dw_ref, abuf, mbuf,
    ld_ref, ad_ref, md_ref, basis_ref, lbuf, eh, el, bas, dd, drecv, f2, frecv, fsum, xt_ref, m_ref, mrecv1, mrecv2, msum, mrecv3, mz,
    gsend, grecv, gz, gram,
    small_sem, lsem, asem, msem, ssem, rsem,
):
    rep = lax.axis_index("rep")
    shard = lax.axis_index("shard")
    z, core = shard // CORES, shard % CORES
    other = 1 - core
    width = lbuf.shape[2]
    rank = basis_ref.shape[0]

    def rep_dev(j):
        return ((rep + j) % GROUPS, shard)

    def z_dev(j):
        return (rep, ((z + j) % GROUPS) * CORES + core)

    core_dev = (rep, z * CORES + other)
    started = []

    def send(src, dst, dev):
        i = len(started)
        copy = pltpu.make_async_remote_copy(
            src_ref=src, dst_ref=dst, send_sem=ssem.at[i], recv_sem=rsem.at[i],
            device_id=dev, device_id_type=MESH,
        )
        copy.start()
        started.append(copy)
        return copy

    small = [
        pltpu.make_async_copy(src, dst, small_sem.at[i])
        for i, (src, dst) in enumerate(
            ((basis_hbm, basis_ref), (ld_hbm, ld_ref), (ad_hbm, ad_ref), (md_hbm, md_ref))
        )
    ]
    for copy in small:
        copy.start()
    differences = ((local_hbm, lbuf, lsem), (anchor_hbm, abuf, asem))
    momenta = ((momentum_hbm, mbuf, msem),)

    def load(k, start, arrays=differences):
        cols = pl.ds(pl.multiple_of(k * width, width), width)
        for src, dst, sem in arrays:
            copy = pltpu.make_async_copy(src.at[:, cols], dst.at[k], sem.at[k])
            if start:
                copy.start()
            else:
                copy.wait()

    @pl.loop(0, CHUNKS)
    def _(k):
        load(k, True)

    barrier = pltpu.get_barrier_semaphore()
    peers = [core_dev] + [rep_dev(j) for j in (1, 2, 3)] + [z_dev(j) for j in (1, 2, 3)]
    for dev in peers:
        pl.semaphore_signal(barrier, inc=1, device_id=dev, device_id_type=MESH)

    for copy in small:
        copy.wait()
    b = basis_ref[...].T
    b_hi = b.astype(bf16)
    b_lo = (b - b_hi.astype(f32)).astype(bf16)
    bas[shard] = jnp.concatenate([b_hi, b_lo], axis=1)
    dd[...] = ad_ref[...] - ld_ref[...]
    pl.semaphore_wait(barrier, len(peers))

    basis_z = [send(bas.at[shard], bas.at[shard], z_dev(j)) for j in (1, 2, 3)]
    basis_core = [send(bas.at[shard], bas.at[shard], core_dev)]
    dense_rs = [send(dd.at[(rep + j) % GROUPS], drecv.at[j - 1], rep_dev(j)) for j in (1, 2, 3)]

    def split(k):
        load(k, False)
        e = abuf[k] - lbuf[k]
        hi = e.astype(bf16)
        eh[k] = hi
        el[k] = (e - hi.astype(f32)).astype(bf16)

    pl.loop(0, CHUNKS - 2)(split)
    for j in (1, 2, 3):
        basis_z[j - 1].wait_recv()
        at = ((z + GROUPS - j) % GROUPS) * CORES + core
        basis_core.append(send(bas.at[at], bas.at[at], core_dev))
    pl.loop(CHUNKS - 2, CHUNKS)(split)

    @pl.loop(0, CHUNKS)
    def _(k):
        load(k, True, momenta)

    for copy in basis_core:
        copy.wait_recv()

    half = f2.shape[0] * f2.shape[1]
    lanes = f2.shape[2]
    piece = f2.shape[1]

    def summed(start):
        total = jnp.zeros((half, lanes), f32)
        for k in range(CHUNKS):
            total += jnp.dot(eh[k, start : start + half, :], bas[k], preferred_element_type=f32)
            total += jnp.dot(el[k, start : start + half, :], bas[k], preferred_element_type=f32)
        return total + pltpu.roll(total, rank, 1)

    lane_f = lax.broadcasted_iota(jnp.int32, (half, lanes), 1)
    f2[...] = jnp.where(lane_f < rank, summed(0), summed(half)).reshape(f2.shape)

    factor_rs = [send(f2.at[(rep + j) % GROUPS], frecv.at[j - 1], rep_dev(j)) for j in (1, 2, 3)]

    for copy in dense_rs:
        copy.wait_recv()
    dg_ref[rep] = (dd[rep] + drecv[0] + drecv[1] + drecv[2]) / GROUPS
    new_dense, _ = nesterov(dg_ref[rep], ad_ref[rep], md_ref[rep])
    dw_ref[core, rep, z] = new_dense.astype(bf16)

    for copy in factor_rs:
        copy.wait_recv()
    fsum[rep] = f2[rep] + frecv[0] + frecv[1] + frecv[2]
    factor_ag = [send(fsum.at[rep], fsum.at[rep], rep_dev(j)) for j in (1, 2, 3)]
    dense_ag = [send(dg_ref.at[rep], dg_ref.at[rep], rep_dev(j)) for j in (1, 2, 3)]
    mine = dw_ref.at[core, rep, z]
    weights_z = [send(mine, mine, z_dev(j)) for j in (1, 2, 3)]
    for copy in factor_ag:
        copy.wait_recv()

    lane = lax.broadcasted_iota(jnp.int32, (piece, lanes), 1)
    for q in range(GROUPS):
        here = fsum[q]
        there = pltpu.roll(here, rank, 1)
        for top, twice in ((0, jnp.where(lane < rank, here, there)), (half, jnp.where(lane < rank, there, here))):
            hi = twice.astype(bf16).astype(f32)
            x = jnp.where(lane < rank, hi, twice - hi)
            at = top + q * piece
            x_ref[at : at + piece, :] = x.astype(bf16)
            xt_ref[:, at : at + piece] = x.T.astype(bf16)

    g = jnp.dot(xt_ref[...], x_ref[...], preferred_element_type=f32)
    g = g[:rank] + g[rank:]
    g = g + pltpu.roll(g, rank, 1)
    fold = rank // 2
    lane_g = lax.broadcasted_iota(jnp.int32, (fold, lanes), 1)
    gsend[...] = jnp.where(lane_g < rank, g[:fold], g[fold:])
    gram_core = send(gsend, grecv, core_dev)

    def coefficient(k):
        m = jnp.dot(xt_ref[...], eh[k], preferred_element_type=f32)
        m += jnp.dot(xt_ref[...], el[k], preferred_element_type=f32)
        m_ref[k] = m[:rank] + m[rank:]

    @pl.loop(0, GROUPS)
    def _(i):
        coefficient(other * GROUPS + i)

    coeff_core = send(m_ref.at[pl.ds(other * GROUPS, GROUPS)], mrecv1, core_dev)

    @pl.loop(0, GROUPS)
    def _(i):
        coefficient(core * GROUPS + i)

    gram_core.wait_recv()
    gz[z] = gsend[...] + grecv[...]
    gram_z = [send(gz.at[z], gz.at[z], z_dev(j)) for j in (1, 2, 3)]

    coeff_core.wait_recv()
    mrecv1[...] += m_ref[pl.ds(core * GROUPS, GROUPS)]
    coeff_rs = [send(mrecv1.at[(rep + j) % GROUPS], mrecv2.at[j - 1], rep_dev(j)) for j in (1, 2, 3)]

    for copy in weights_z:
        copy.wait_recv()
    first, second = pl.ds(0, GROUPS // 2), pl.ds(GROUPS // 2, GROUPS // 2)
    ours = dw_ref.at[core, rep, first]
    weights_first = [send(ours, ours, rep_dev(j)) for j in (1, 2, 3)]
    ours = dw_ref.at[core, rep, second]
    weights_second = [send(ours, ours, rep_dev(j)) for j in (1, 2, 3)]

    for copy in gram_z:
        copy.wait_recv()
    folded = gz[0] + gz[1] + gz[2] + gz[3]
    back = pltpu.roll(folded, rank, 1)
    gram[:fold] = folded
    gram[fold:] = back

    sub_i = lax.broadcasted_iota(jnp.int32, (rank, lanes), 0)
    lane_i = lax.broadcasted_iota(jnp.int32, (rank, lanes), 1)
    lane_1 = lax.broadcasted_iota(jnp.int32, (1, lanes), 1)

    def pick(values, at):
        return jnp.sum(jnp.where(at, values, 0.0), axis=1, keepdims=True)

    def eliminate_two(pair):
        k = pair * 2
        a = gram[...]
        row0, row1 = gram[pl.ds(k, 1), :], gram[pl.ds(k + 1, 1), :]
        at0, at1 = lane_i == k, lane_i == k + 1
        one0, one1 = lane_1 == k, lane_1 == k + 1
        col0, col1 = pick(a, at0), pick(a, at1)
        s00, s01, s10, s11 = pick(row0, one0), pick(row0, one1), pick(row1, one0), pick(row1, one1)
        p0 = jnp.where(one0, 1.0, row0) / s00
        q01 = s01 / s00
        row1 = jnp.where(one0, 0.0, row1) - s10 * p0
        p1 = jnp.where(one1, 1.0, row1) / (s11 - s10 * q01)
        p0 = jnp.where(one1, 0.0, p0)
        col1 = col1 - col0 * q01
        rest = jnp.where(at0 | at1, 0.0, a) - col0 * p0 - col1 * p1
        gram[...] = jnp.where(sub_i == k, p0 - q01 * p1, jnp.where(sub_i == k + 1, p1, rest))

    pl.loop(0, rank // 4)(eliminate_two)
    for copy in coeff_rs:
        copy.wait_recv()
    msum[...] = (mrecv1[rep] + mrecv2[0] + mrecv2[1] + mrecv2[2]).reshape(msum.shape)
    coeff_z = [send(msum.at[(z + j) % GROUPS], mrecv3.at[j - 1], z_dev(j)) for j in (1, 2, 3)]
    pl.loop(rank // 4, 3 * rank // 8)(eliminate_two)
    for copy in coeff_z:
        copy.wait_recv()
    mz[z] = msum[z] + mrecv3[0] + mrecv3[1] + mrecv3[2]
    coeff_zag = [send(mz.at[z], mz.at[z], z_dev(j)) for j in (1, 2, 3)]
    pl.loop(3 * rank // 8, rank // 2)(eliminate_two)
    for copy in coeff_zag:
        copy.wait_recv()
    h = jnp.dot(gram[:, :rank], mz[...].reshape(rank, width), precision=highest, preferred_element_type=f32)
    h = h / GROUPS
    h_hi = h.astype(bf16)
    own = core * GROUPS + rep
    h_ref[own, :rank, :] = h_hi
    h_ref[own, rank:, :] = (h - h_hi.astype(f32)).astype(bf16)
    h_rep = [send(h_ref.at[own], h_ref.at[own], rep_dev(j)) for j in (1, 2, 3)]
    h_core = [send(h_ref.at[own], h_ref.at[own], core_dev)]
    for j in (1, 2, 3):
        h_rep[j - 1].wait_recv()
        at = core * GROUPS + (rep + GROUPS - j) % GROUPS
        h_core.append(send(h_ref.at[at], h_ref.at[at], core_dev))

    weights_core = []
    for part, arrivals in ((first, weights_first), (second, weights_second)):
        for copy in arrivals:
            copy.wait_recv()
        here = dw_ref.at[core, :, part]
        weights_core.append(send(here, here, core_dev))
    for copy in dense_ag + h_core + weights_core:
        copy.wait_recv()

    @pl.loop(0, CHUNKS)
    def _(k):
        load(k, False, momenta)

    for copy in started:
        copy.wait_send()


def update_kernel(x_ref, h_ref, anchor_ref, mom_ref, dg_ref, ad_ref, md_ref, dw_ref,
                  dn_out, dm_out, dw_out, new_out, mom_out, nbuf, pbuf, nsem, psem, wsem):
    rank = h_ref.shape[1] // 2
    width = h_ref.shape[2]
    def weights(at):
        return pltpu.make_async_copy(
            dw_ref.at[at % CORES, :, at // CORES], dw_out.at[at // CORES, at % CORES], wsem.at[at]
        )

    def out(k):
        cols = pl.ds(pl.multiple_of(k * width, width), width)
        return (
            pltpu.make_async_copy(nbuf.at[k % 2], new_out.at[:, cols], nsem.at[k % 2]),
            pltpu.make_async_copy(pbuf.at[k % 2], mom_out.at[:, cols], psem.at[k % 2]),
        )

    for at in range(CHUNKS):
        weights(at).start()
    x2 = jnp.concatenate([x_ref[...], x_ref[...]], axis=1)

    @pl.loop(0, CHUNKS)
    def _(k):
        hi, lo = h_ref[k, :rank, :], h_ref[k, rank:, :]
        right = jnp.concatenate([hi, hi, lo, lo], axis=0)

        @pl.when(k >= 2)
        def _():
            for copy in out(k - 2):
                copy.wait()

        grad = jnp.dot(x2, right, preferred_element_type=f32)
        nbuf[k % 2], pbuf[k % 2] = nesterov(grad, anchor_ref[k], mom_ref[k])
        for copy in out(k):
            copy.start()

    dn_out[...], dm_out[...] = nesterov(dg_ref[...], ad_ref[...], md_ref[...])
    for k in (CHUNKS - 2, CHUNKS - 1):
        for copy in out(k):
            copy.wait()
    for at in range(CHUNKS):
        weights(at).wait()


def fused(local_dense, anchor_dense, momentum_dense, local_emb, anchor_emb, momentum_emb, proj_basis):
    rows, cols = anchor_emb.shape
    drows, dcols = anchor_dense.shape
    rank = proj_basis.shape[1]
    width = cols // CHUNKS
    dq = drows // GROUPS
    piece = rows // 2 // GROUPS
    lanes = 2 * rank
    quarters = (GROUPS, dq, dcols)
    vmem = pl.BlockSpec(memory_space=pltpu.VMEM)
    hbm = pl.BlockSpec(memory_space=pltpu.HBM)
    S = jax.ShapeDtypeStruct
    stay = lambda array: pltpu.with_memory_space_constraint(array, pltpu.HBM)
    h, x, dg, dw, anchor, momentum = pl.pallas_call(
        exchange_kernel,
        out_shape=(
            S((CHUNKS, lanes, width), bf16),
            S((rows, lanes), bf16),
            S(quarters, f32),
            S((CORES, GROUPS, GROUPS, dq, dcols), bf16),
            S((CHUNKS, rows, width), f32),
            S((CHUNKS, rows, width), f32),
        ),
        in_specs=[hbm] * 7,
        out_specs=(vmem,) * 6,
        scratch_shapes=[
            pltpu.VMEM(quarters, f32),
            pltpu.VMEM(quarters, f32),
            pltpu.VMEM(quarters, f32),
            pltpu.VMEM((rank, width), f32),
            pltpu.VMEM((CHUNKS, rows, width), f32),
            pltpu.VMEM((CHUNKS, rows, width), bf16),
            pltpu.VMEM((CHUNKS, rows, width), bf16),
            pltpu.VMEM((CHUNKS, width, lanes), bf16),
            pltpu.VMEM(quarters, f32),
            pltpu.VMEM((3, dq, dcols), f32),
            pltpu.VMEM((GROUPS, piece, lanes), f32),
            pltpu.VMEM((3, piece, lanes), f32),
            pltpu.VMEM((GROUPS, piece, lanes), f32),
            pltpu.VMEM((lanes, rows), bf16),
            pltpu.VMEM((CHUNKS, rank, width), f32),
            pltpu.VMEM((GROUPS, rank, width), f32),
            pltpu.VMEM((3, rank, width), f32),
            pltpu.VMEM((GROUPS, rank // GROUPS, width), f32),
            pltpu.VMEM((3, rank // GROUPS, width), f32),
            pltpu.VMEM((GROUPS, rank // GROUPS, width), f32),
            pltpu.VMEM((rank // 2, lanes), f32),
            pltpu.VMEM((rank // 2, lanes), f32),
            pltpu.VMEM((GROUPS, rank // 2, lanes), f32),
            pltpu.VMEM((rank, lanes), f32),
            pltpu.SemaphoreType.DMA((4,)),
            pltpu.SemaphoreType.DMA((CHUNKS,)),
            pltpu.SemaphoreType.DMA((CHUNKS,)),
            pltpu.SemaphoreType.DMA((CHUNKS,)),
            pltpu.SemaphoreType.DMA((N_COPIES,)),
            pltpu.SemaphoreType.DMA((N_COPIES,)),
        ],
        compiler_params=pltpu.CompilerParams(
            collective_id=0, has_side_effects=True, vmem_limit_bytes=LIMIT1
        ),
    )(
        local_emb[0], anchor_emb, momentum_emb, stay(local_dense[0].reshape(quarters)),
        stay(anchor_dense.reshape(quarters)), stay(momentum_dense.reshape(quarters)), stay(proj_basis.T),
    )

    dn, dm, weights, new, mom = pl.pallas_call(
        update_kernel,
        out_shape=(
            S(anchor_dense.shape, f32),
            S(anchor_dense.shape, f32),
            S((GROUPS, CORES, GROUPS, dq, dcols), bf16),
            S(anchor_emb.shape, f32),
            S(anchor_emb.shape, f32),
        ),
        in_specs=[vmem] * 8,
        out_specs=(vmem, vmem, hbm, hbm, hbm),
        scratch_shapes=[
            pltpu.VMEM((2, rows, width), f32),
            pltpu.VMEM((2, rows, width), f32),
            pltpu.SemaphoreType.DMA((2,)),
            pltpu.SemaphoreType.DMA((2,)),
            pltpu.SemaphoreType.DMA((CHUNKS,)),
        ],
        compiler_params=pltpu.CompilerParams(vmem_limit_bytes=LIMIT2),
    )(x, h, anchor, momentum, dg.reshape(anchor_dense.shape), anchor_dense, momentum_dense, dw)
    return dn, dm, weights.reshape(drows * CHUNKS, dcols), new, mom


def solution(mesh):
    fits = mesh.shape["rep"] == GROUPS and mesh.shape["shard"] == CHUNKS
    placed = (
        P("rep", "shard", None),
        P("shard", None),
        P("shard", None),
        P("rep", "shard", None),
        P("shard", None),
        P("shard", None),
        P("shard", None),
    )
    return jax.shard_map(
        fused if fits else plain,
        mesh=mesh,
        in_specs=placed,
        out_specs=(P("shard", None), P("shard", None), P(), P("shard", None), P("shard", None)),
        check_vma=False,
    )
```
